32 devices in a mesh: ctx: 2 (over x), row: 4 (over y, core), col: 4 (over z).
Axes of the slice: x: 2, y: 2, z: 4, core: 2. Of those that a mesh axis runs over, the one named last changes fastest.
Arguments:
- activations: bfloat16 [2048, 4096], P('ctx', 'col'), may hold values from -640 to 640
- norm_gain: float32 [4096], P('col'), may hold values from 0.1 to 1.9
- w_query: bfloat16 [4096, 4096], P(('row', 'ctx'), 'col'), may hold values from -0.09375 to 0.09375
- w_key: bfloat16 [4096, 4096], P(('row', 'ctx'), 'col'), may hold values from -0.09375 to 0.09375
- w_value: bfloat16 [4096, 4096], P(('row', 'ctx'), 'col'), may hold values from -0.09375 to 0.09375
- short_taps: float32 [3, 3, 4096], P(None, None, ('row', 'col')), may hold values from -2.5 to 2.5
- long_taps: float32 [128, 4096], P(None, ('row', 'col')), may hold values from -0.5 to 0.5
- skip_gain: float32 [4096], P(('row', 'col')), may hold values from -4 to 4
- w_out: bfloat16 [4096, 4096], P(('col', 'ctx'), 'row'), may hold values from -0.09375 to 0.09375
Outputs:
- mixer_out: bfloat16 [2048, 4096], P(('ctx', 'row'), 'col')
The draws below stay inside these ranges and needn't reach their ends.
All inputs are finite; a program needn't handle non-finite values.
Results may differ from the reference program's by a relative error of at most 0.03.
Values may be sent and summed in bfloat16 or wider, within the bound.
A program may use at most 128 MiB of HBM per device.

```python
import jax
import jax.numpy as jnp
from jax import lax

D = 4096
C = 4096
SHORT_LEN = 3
FILTER_LEN = 128
TOKENS = 2048
N_ROW = 4
N_COL = 4


def draw_activations(key, part):
    first_key, second_key = jax.random.split(key, 2)
    column_scale = jnp.power(10.0, jnp.arange(D, dtype=jnp.float32) / (D - 1))
    base_vals = jax.random.normal(first_key, (TOKENS, D), jnp.float32)
    row_scale = jnp.exp(jax.random.uniform(second_key, (TOKENS, 1), jnp.float32, 0.0, jnp.log(10.0)))
    base_vals = jnp.clip(base_vals, -4.0, 4.0)
    return (base_vals * column_scale[None, :] * row_scale).astype(jnp.bfloat16)


def level_of(own_key, dims, cuts, low, top_value):
    factor_of, own = 1.0, jax.random.fold_in(own_key, 6)
    for dim, parts in cuts:
        draws = jnp.exp(jax.random.uniform(jax.random.fold_in(own, dim), (parts,), jnp.float32, low / len(cuts), top_value / len(cuts)))
        factor_of = factor_of * jnp.repeat(draws, dims[dim] // parts).reshape([-1 if axis == dim else 1 for axis in range(len(dims))])
    return factor_of


def normal_values(rng, dims, width, most, pieces=(), held_as=jnp.bfloat16):
    level = level_of(rng, dims, pieces, -0.22, 0.18) if pieces else 1.0
    entries = jax.random.normal(rng, dims, jnp.float32) * width * level
    return jnp.minimum(jnp.maximum(entries, -most), most).astype(held_as)


def setup_inputs(seed: int = 0) -> dict:
    splits = jax.random.split(jax.random.key(seed), 10)
    activations = draw_activations(jax.random.fold_in(splits[9], 71), 0)
    norm_gain = jnp.clip(1.0 + 0.18 * jax.random.normal(splits[1], (D,), jnp.float32), 0.1, 1.9)
    w_query = normal_values(splits[2], (C, D), D ** -0.5, 0.09375, ((0, 8), (1, 4)))
    w_key = normal_values(splits[3], (C, D), D ** -0.5, 0.09375, ((0, 8), (1, 4)))
    w_value = normal_values(splits[4], (C, D), D ** -0.5, 0.09375, ((0, 8), (1, 4)))
    short_taps = normal_values(splits[5], (3, SHORT_LEN, C), 0.4, 2.5, ((2, 16),), jnp.float32)
    long_taps = normal_values(splits[6], (FILTER_LEN, C), FILTER_LEN ** -0.5, 0.5, ((1, 16),), jnp.float32)
    skip_gain = normal_values(splits[7], (C,), 1.0, 4.0, ((0, 16),), jnp.float32)
    w_out = normal_values(splits[8], (D, C), C ** -0.5, 0.09375, ((0, 8), (1, 4)))
    return {"activations": activations, "norm_gain": norm_gain, "w_query": w_query, "w_key": w_key, "w_value": w_value, "short_taps": short_taps, "long_taps": long_taps, "skip_gain": skip_gain, "w_out": w_out}


epsilon = 1e-05

def causal_filter(signal, tap_vals):
    tap_count = tap_vals.shape[0]
    kernel = jnp.transpose(jnp.flip(tap_vals, axis=0))[:, None, :]
    result = lax.conv_general_dilated(signal[None], kernel, (1,), [(tap_count - 1, 0)], dimension_numbers=('NCH', 'OIH', 'NCH'), feature_group_count=signal.shape[0], precision=lax.Precision.HIGHEST)
    return result[0]

def reference(activations, norm_gain, w_query, w_key, w_value, short_taps, long_taps, skip_gain, w_out):
    as_float = activations.astype(jnp.float32)
    squares = lax.optimization_barrier(jnp.sum(as_float * as_float, axis=1, keepdims=True))
    normed = (as_float * lax.rsqrt(squares / D + epsilon) * norm_gain).astype(jnp.bfloat16)
    quarter = D // N_COL
    token_count = normed.shape[0]
    group_size = min(C, 256)
    group_count = C // group_size

    def project(weight_rows):
        running = jnp.zeros((weight_rows.shape[0], token_count), jnp.float32)
        for block_idx in range(N_COL):
            part_sum = lax.dot_general(weight_rows[:, block_idx * quarter:(block_idx + 1) * quarter], normed[:, block_idx * quarter:(block_idx + 1) * quarter], (((1,), (1,)), ((), ())), preferred_element_type=jnp.float32)
            running = running + lax.optimization_barrier(part_sum.astype(jnp.bfloat16)).astype(jnp.float32)
        return running.astype(jnp.bfloat16)

    def channel_group(operands):
        query_rows, key_rows, value_rows, short_group, long_group, skip_group = operands
        query_vals = causal_filter(project(query_rows).astype(jnp.float32), short_group[0])
        key_vals = causal_filter(project(key_rows).astype(jnp.float32), short_group[1])
        value_vals = causal_filter(project(value_rows).astype(jnp.float32), short_group[2])
        gate_vals = key_vals * value_vals
        long_part = causal_filter(gate_vals, long_group)
        return (query_vals * (long_part + skip_group[:, None] * gate_vals)).astype(jnp.bfloat16)
    mixed_all = lax.map(channel_group, (w_query.reshape(group_count, group_size, D), w_key.reshape(group_count, group_size, D), w_value.reshape(group_count, group_size, D), jnp.moveaxis(short_taps.reshape(3, SHORT_LEN, group_count, group_size), 2, 0), jnp.moveaxis(long_taps.reshape(FILTER_LEN, group_count, group_size), 1, 0), skip_gain.reshape(group_count, group_size)))
    mixed_all = mixed_all.reshape(C, token_count)
    fourth = C // N_ROW
    running = jnp.zeros((token_count, D), jnp.float32)
    for block_idx in range(N_ROW):
        part_sum = lax.dot_general(mixed_all[block_idx * fourth:(block_idx + 1) * fourth], w_out[:, block_idx * fourth:(block_idx + 1) * fourth], (((0,), (1,)), ((), ())), preferred_element_type=jnp.float32)
        running = running + lax.optimization_barrier(part_sum.astype(jnp.bfloat16)).astype(jnp.float32)
    return running.astype(jnp.bfloat16)
```

```python
import functools

import jax
import jax.numpy as jnp
from jax import lax
from jax.experimental import pallas as pl
from jax.experimental.pallas import tpu as pltpu
from jax.sharding import PartitionSpec as P

D = 4096
SHORT_LEN = 3
FILTER_LEN = 128
SUB = 8
epsilon = 1e-05


def filter_kernel(x_ref, scale_ref, short_ref, long_ref, skip_ref, out_ref, prev, gates, shifted):
    step = pl.program_id(0)
    rows = x_ref.shape[1]

    @pl.when(step == 0)
    def _():
        prev[...] = jnp.zeros_like(prev)
        gates[0:SUB, :] = jnp.zeros((SUB, gates.shape[1]), jnp.float32)
        shifted[:, 0:FILTER_LEN, :] = jnp.zeros((SUB, FILTER_LEN, shifted.shape[2]), jnp.float32)

    @pl.when(step > 0)
    def _():
        shifted[:, 0:FILTER_LEN, :] = shifted[:, rows : rows + FILTER_LEN, :]

    filtered = []
    for which in range(3):
        now = x_ref[which].astype(jnp.float32) * scale_ref[...]
        prev[which, SUB:, :] = now
        total = short_ref[which, 0:1, :] * now
        for tap in range(1, SHORT_LEN):
            total = total + short_ref[which, tap : tap + 1, :] * prev[which, SUB - tap : SUB - tap + rows, :]
        filtered.append(total)
        prev[which, 0:SUB, :] = prev[which, rows : rows + SUB, :]
    gate = filtered[1] * filtered[2]
    gates[SUB:, :] = gate
    for move in range(SUB):
        shifted[move, FILTER_LEN:, :] = gates[SUB - move : SUB - move + rows, :]
    gates[0:SUB, :] = gates[rows : rows + SUB, :]
    total = skip_ref[...] * gate
    for move in range(SUB):
        for back in range(0, FILTER_LEN, SUB):
            total = total + long_ref[back + move : back + move + 1, :] * shifted[
                move, FILTER_LEN - back : FILTER_LEN - back + rows, :
            ]
    out_ref[...] = (filtered[0] * total).astype(out_ref.dtype)


def mix(stacked, scale, short_taps, long_taps, skip_gain):
    _, tokens, channels = stacked.shape
    rows = FILTER_LEN
    return pl.pallas_call(
        filter_kernel,
        grid=(tokens // rows,),
        in_specs=[
            pl.BlockSpec((3, rows, channels), lambda i: (0, i, 0)),
            pl.BlockSpec((rows, 1), lambda i: (i, 0)),
            pl.BlockSpec((3, SHORT_LEN, channels), lambda i: (0, 0, 0)),
            pl.BlockSpec((FILTER_LEN, channels), lambda i: (0, 0)),
            pl.BlockSpec((1, channels), lambda i: (0, 0)),
        ],
        out_specs=pl.BlockSpec((rows, channels), lambda i: (i, 0)),
        out_shape=jax.ShapeDtypeStruct((tokens, channels), jnp.bfloat16),
        scratch_shapes=[
            pltpu.VMEM((3, SUB + rows, channels), jnp.float32),
            pltpu.VMEM((SUB + rows, channels), jnp.float32),
            pltpu.VMEM((SUB, FILTER_LEN + rows, channels), jnp.float32),
        ],
    )(stacked, scale, short_taps, long_taps, skip_gain)


def shift(value, axis, size, by):
    return lax.ppermute(value, axis, [((i + by) % size, i) for i in range(size)])


def on_device(
    n_ctx, n_row, n_col,
    activations, norm_gain, w_query, w_key, w_value, short_taps, long_taps, skip_gain, w_out,
):
    ctx, col = lax.axis_index("ctx"), lax.axis_index("col")
    tokens, features = activations.shape
    held = w_query.shape[0]
    width = held // n_col
    stacked = jnp.stack([w_query, w_key, w_value]).reshape(3, n_col, width, features)

    taps = jnp.concatenate([short_taps.reshape(9, -1), long_taps, skip_gain[None]], axis=0)
    taps = lax.all_gather(taps, "col", axis=1, tiled=True)
    taps = lax.dynamic_slice_in_dim(taps, ctx * held + col * width, width, 1)

    w_full = lax.all_gather(w_out, "ctx", axis=0, tiled=True)
    w_full = jnp.transpose(w_full.reshape(-1, n_ctx, n_col, width), (0, 2, 1, 3)).reshape(w_full.shape)

    qkv = jnp.zeros((3, n_ctx * tokens, width), jnp.bfloat16)
    squares = jnp.zeros((n_ctx * tokens,), jnp.float32)
    for step in range(n_ctx):
        part = activations if step == 0 else shift(activations, "ctx", n_ctx, step)
        first = lax.rem(ctx + step, n_ctx) * tokens
        as_float = part.astype(jnp.float32)
        squares = lax.dynamic_update_slice(squares, jnp.sum(as_float * as_float, axis=1), (first,))
        scaled = (as_float * norm_gain).astype(jnp.bfloat16)
        partial_value = jnp.einsum("td,skcd->kstc", scaled, stacked, preferred_element_type=jnp.float32)
        summed = lax.psum_scatter(partial_value.astype(jnp.bfloat16), "col", scatter_dimension=0, tiled=True)
        qkv = lax.dynamic_update_slice(qkv, summed[0], (0, first, 0))

    total = squares.reshape(-1, 128)
    for step in range(1, n_col):
        total = total + shift(squares.reshape(-1, 128), "col", n_col, step)
    scale = lax.rsqrt(total / D + epsilon).reshape(-1, 1)

    mixed = mix(qkv, scale, taps[:9].reshape(3, 3, width), taps[9:-1], taps[-1:])

    spread = lax.all_to_all(
        mixed.reshape(n_ctx, tokens, width), "ctx", split_axis=0, concat_axis=0, tiled=True
    )
    spread = jnp.transpose(spread, (1, 0, 2)).reshape(tokens, n_ctx * width)
    block_rows = lax.all_gather(spread, "col", axis=1, tiled=True)
    out_part = lax.dot_general(
        block_rows, w_full, (((1,), (1,)), ((), ())), preferred_element_type=jnp.float32
    )
    return lax.psum_scatter(out_part.astype(jnp.bfloat16), "row", scatter_dimension=0, tiled=True)


def solution(mesh):
    in_specs = (
        P("ctx", "col"),
        P("col"),
        P(("row", "ctx"), "col"),
        P(("row", "ctx"), "col"),
        P(("row", "ctx"), "col"),
        P(None, None, ("row", "col")),
        P(None, ("row", "col")),
        P(("row", "col")),
        P(("col", "ctx"), "row"),
    )
    out_specs = P(("ctx", "row"), "col")
    body = functools.partial(on_device, mesh.shape["ctx"], mesh.shape["row"], mesh.shape["col"])
    return jax.shard_map(body, mesh=mesh, in_specs=in_specs, out_specs=out_specs, check_vma=False)
```

```python
import functools

import jax
import jax.numpy as jnp
from jax import lax
from jax.experimental import pallas as pl
from jax.experimental.pallas import tpu as pltpu
from jax.sharding import PartitionSpec as P

D = 4096
SHORT_LEN = 3
FILTER_LEN = 128
SUB = 8
epsilon = 1e-05


def filter_kernel(x_ref, scale_ref, short_ref, long_ref, skip_ref, out_ref, prev, gates, shifted):
    step = pl.program_id(0)
    rows = x_ref.shape[1]

    @pl.when(step == 0)
    def _():
        prev[...] = jnp.zeros_like(prev)
        gates[0:SUB, :] = jnp.zeros((SUB, gates.shape[1]), jnp.float32)
        shifted[:, 0:FILTER_LEN, :] = jnp.zeros((SUB, FILTER_LEN, shifted.shape[2]), jnp.float32)

    @pl.when(step > 0)
    def _():
        shifted[:, 0:FILTER_LEN, :] = shifted[:, rows : rows + FILTER_LEN, :]

    filtered = []
    for which in range(3):
        now = x_ref[which].astype(jnp.float32) * scale_ref[...]
        prev[which, SUB:, :] = now
        total = short_ref[which, 0:1, :] * now
        for tap in range(1, SHORT_LEN):
            total = total + short_ref[which, tap : tap + 1, :] * prev[which, SUB - tap : SUB - tap + rows, :]
        filtered.append(total)
        prev[which, 0:SUB, :] = prev[which, rows : rows + SUB, :]
    gate = filtered[1] * filtered[2]
    gates[SUB:, :] = gate
    for move in range(SUB):
        shifted[move, FILTER_LEN:, :] = gates[SUB - move : SUB - move + rows, :]
    gates[0:SUB, :] = gates[rows : rows + SUB, :]
    total = skip_ref[...] * gate
    for move in range(SUB):
        for back in range(0, FILTER_LEN, SUB):
            total = total + long_ref[back + move : back + move + 1, :] * shifted[
                move, FILTER_LEN - back : FILTER_LEN - back + rows, :
            ]
    out_ref[...] = (filtered[0] * total).astype(out_ref.dtype)


def mix(stacked, scale, short_taps, long_taps, skip_gain):
    _, tokens, channels = stacked.shape
    rows = FILTER_LEN
    return pl.pallas_call(
        filter_kernel,
        grid=(tokens // rows,),
        in_specs=[
            pl.BlockSpec((3, rows, channels), lambda i: (0, i, 0)),
            pl.BlockSpec((rows, 1), lambda i: (i, 0)),
            pl.BlockSpec((3, SHORT_LEN, channels), lambda i: (0, 0, 0)),
            pl.BlockSpec((FILTER_LEN, channels), lambda i: (0, 0)),
            pl.BlockSpec((1, channels), lambda i: (0, 0)),
        ],
        out_specs=pl.BlockSpec((rows, channels), lambda i: (i, 0)),
        out_shape=jax.ShapeDtypeStruct((tokens, channels), jnp.bfloat16),
        scratch_shapes=[
            pltpu.VMEM((3, SUB + rows, channels), jnp.float32),
            pltpu.VMEM((SUB + rows, channels), jnp.float32),
            pltpu.VMEM((SUB, FILTER_LEN + rows, channels), jnp.float32),
        ],
    )(stacked, scale, short_taps, long_taps, skip_gain)


def shift(value, axis, size, by):
    return lax.ppermute(value, axis, [((i + by) % size, i) for i in range(size)])


def on_device(
    n_ctx, n_row, n_col,
    activations, norm_gain, w_query, w_key, w_value, short_taps, long_taps, skip_gain, w_out,
):
    ctx, col = lax.axis_index("ctx"), lax.axis_index("col")
    tokens, features = activations.shape
    held = w_query.shape[0]
    width = held // n_col
    stacked = jnp.stack([w_query, w_key, w_value]).reshape(3, n_col, width, features)

    taps = jnp.concatenate([short_taps.reshape(9, -1), long_taps, skip_gain[None]], axis=0)
    taps = lax.all_gather(taps, "col", axis=1, tiled=True)
    taps = lax.dynamic_slice_in_dim(taps, ctx * held + col * width, width, 1)

    w_full = lax.all_gather(w_out, "ctx", axis=0, tiled=True)
    w_full = jnp.transpose(w_full.reshape(-1, n_ctx, n_col, width), (0, 2, 1, 3)).reshape(w_full.shape)

    qkv = jnp.zeros((3, n_ctx * tokens, width), jnp.bfloat16)
    squares = jnp.zeros((n_ctx * tokens,), jnp.float32)
    for step in range(n_ctx):
        part = activations if step == 0 else shift(activations, "ctx", n_ctx, step)
        first = lax.rem(ctx + step, n_ctx) * tokens
        as_float = part.astype(jnp.float32)
        squares = lax.dynamic_update_slice(squares, jnp.sum(as_float * as_float, axis=1), (first,))
        scaled = (as_float * norm_gain).astype(jnp.bfloat16)
        partial_value = jnp.einsum("td,skcd->kstc", scaled, stacked, preferred_element_type=jnp.float32)
        summed = lax.psum_scatter(partial_value.astype(jnp.bfloat16), "col", scatter_dimension=0, tiled=True)
        qkv = lax.dynamic_update_slice(qkv, summed[0], (0, first, 0))

    total = squares.reshape(-1, 128)
    for step in range(1, n_col):
        total = total + shift(squares.reshape(-1, 128), "col", n_col, step)
    scale = lax.rsqrt(total / D + epsilon).reshape(-1, 1)

    mixed = mix(qkv, scale, taps[:9].reshape(3, 3, width), taps[9:-1], taps[-1:])

    spread = lax.all_to_all(
        mixed.reshape(n_ctx, tokens, width), "ctx", split_axis=0, concat_axis=0, tiled=True
    )
    spread = jnp.transpose(spread, (1, 0, 2)).reshape(tokens, n_ctx * width)
    block_rows = lax.all_gather(spread, "col", axis=1, tiled=True)
    out_part = lax.dot_general(
        block_rows, w_full, (((1,), (1,)), ((), ())), preferred_element_type=jnp.float32
    )
    return lax.psum_scatter(out_part.astype(jnp.bfloat16), "row", scatter_dimension=0, tiled=True)


def chain_kernel(
    last, x_ref, gain_ref, w_ref, scale_ref, taps_ref, out_ref,
    xs, acc, prev, gates, shifted, stage, gath,
    acc_send, acc_recv, x_send, x_recv, stage_send, stage_recv, z_send, z_recv,
):
    ctx, col = lax.axis_index("ctx"), lax.axis_index("col")
    pieces = xs.shape[1]
    chunks = acc.shape[1]
    rows = xs.shape[2]
    width = gath.shape[4]
    is_end = (col == 0) | (col == last)
    end_half = jnp.where(col == 0, 0, 1)
    inward = jnp.where(col == 0, 1, last - 1)
    left, right = jnp.maximum(col - 1, 0), jnp.minimum(col + 1, last)
    peer = {"ctx": 1 - ctx}
    mesh_ids = pl.DeviceIdType.MESH

    xs[0] = (x_ref[...].astype(jnp.float32) * gain_ref[...]).astype(jnp.bfloat16).reshape(xs.shape[1:])

    barrier = pltpu.get_barrier_semaphore()
    pl.semaphore_signal(barrier, inc=1, device_id=peer, device_id_type=mesh_ids)

    @pl.when(col > 0)
    def _():
        pl.semaphore_signal(barrier, inc=1, device_id={"col": left}, device_id_type=mesh_ids)

    @pl.when(col < last)
    def _():
        pl.semaphore_signal(barrier, inc=1, device_id={"col": right}, device_id_type=mesh_ids)

    pl.semaphore_wait(barrier, 1 + jnp.where(col > 0, 1, 0) + jnp.where(col < last, 1, 0))

    def x_copy(piece):
        return pltpu.make_async_remote_copy(
            xs.at[0, piece], xs.at[1, piece], x_send.at[piece], x_recv.at[piece],
            device_id=peer, device_id_type=mesh_ids,
        )

    def acc_copy(half, chunk):
        return pltpu.make_async_remote_copy(
            acc.at[half, chunk], acc.at[half, chunk], acc_send.at[half, chunk], acc_recv.at[half, chunk],
            device_id={"col": left if half == 0 else right}, device_id_type=mesh_ids,
        )

    def stage_copy(part):
        return pltpu.make_async_remote_copy(
            stage.at[part], gath.at[end_half, part, ctx], stage_send.at[part], stage_recv.at[part],
            device_id=peer, device_id_type=mesh_ids,
        )

    def z_copy(half, part, source, target):
        return pltpu.make_async_remote_copy(
            gath.at[half, part, source], gath.at[half, part, source],
            z_send.at[half, part, source], z_recv.at[half, part, source],
            device_id={"col": target}, device_id_type=mesh_ids,
        )

    @pl.loop(0, pieces)
    def _(piece):
        x_copy(piece).start()

    def filter_block(part, block):
        mine = lax.rem(block // pieces + ctx, 2)
        chunk = mine * 2 * pieces + part * pieces + lax.rem(block, pieces)
        taps = taps_ref.at[part]
        start = pl.multiple_of(block * rows, rows)
        scale = scale_ref[pl.ds(start, rows), :]

        @pl.when(block == 0)
        def _():
            prev[...] = jnp.zeros_like(prev)
            gates[0:SUB, :] = jnp.zeros((SUB, width), jnp.float32)
            shifted[:, rows:, :] = jnp.zeros((SUB, rows, width), jnp.float32)

        shifted[:, 0:rows, :] = shifted[:, rows:, :]
        filtered = []
        for which in range(3):
            now = acc[end_half, chunk, :, which * width : (which + 1) * width].astype(jnp.float32) * scale
            prev[which, SUB:, :] = now
            total = taps[3 * which : 3 * which + 1, :] * now
            for tap in range(1, SHORT_LEN):
                row = 3 * which + tap
                total = total + taps[row : row + 1, :] * prev[which, SUB - tap : SUB - tap + rows, :]
            filtered.append(total)
            prev[which, 0:SUB, :] = prev[which, rows : rows + SUB, :]
        gate = filtered[1] * filtered[2]
        gates[SUB:, :] = gate
        for move in range(SUB):
            shifted[move, rows:, :] = gates[SUB - move : SUB - move + rows, :]
        gates[0:SUB, :] = gates[rows : rows + SUB, :]
        total = taps[9:10, :] * gate
        for move in range(SUB):
            for back in range(0, FILTER_LEN, SUB):
                row = 16 + back + move
                total = total + taps[row : row + 1, :] * shifted[move, rows - back : 2 * rows - back, :]
        value = (filtered[0] * total).astype(jnp.bfloat16)
        place = pl.ds(pl.multiple_of(lax.rem(block, pieces) * rows, rows), rows)

        @pl.when(mine == 0)
        def _():
            gath[end_half, part, ctx, place, :] = value

        @pl.when(mine == 1)
        def _():
            stage[part, place, :] = value

    def hand_on(part, first):
        @pl.when(is_end & (ctx == first))
        def _():
            z_copy(end_half, part, ctx, inward).start()

        @pl.when(is_end & (ctx != first))
        def _():
            stage_copy(part).start()

    def hand_on_peer(part):
        @pl.when(is_end)
        def _():
            stage_copy(part).wait_recv()
            z_copy(end_half, part, 1 - ctx, inward).start()

    steps = chunks + 2 * last

    @pl.loop(0, steps)
    def _(step):
        first = step - 2 * jnp.minimum(col, last - col)

        @pl.when((first >= 2 * pieces) & (first < 3 * pieces))
        def _():
            x_copy(first - 2 * pieces).wait_recv()

        for half in range(2):
            hops = last - col if half == 0 else col
            chunk = step - 2 * hops

            @pl.when((chunk >= 0) & (chunk < chunks))
            def _():
                part = lax.rem(chunk // pieces, 2)
                own = lax.dot_general(
                    xs[chunk // (2 * pieces), lax.rem(chunk, pieces)], w_ref[2 * half + part],
                    (((1,), (1,)), ((), ())), preferred_element_type=jnp.float32,
                )

                @pl.when(hops == 0)
                def _():
                    acc[half, chunk] = own.astype(jnp.bfloat16)

                @pl.when(hops > 0)
                def _():
                    acc_copy(half, chunk).wait_recv()
                    acc[half, chunk] = (own + acc[half, chunk].astype(jnp.float32)).astype(jnp.bfloat16)

                @pl.when(hops < last)
                def _():
                    acc_copy(half, chunk).start()

        @pl.when(is_end & (step >= steps - pieces))
        def _():
            @pl.loop(0, 2)
            def _(more):
                filter_block(0, 2 * (step - steps + pieces) + more)

    hand_on(0, 0)
    hand_on(0, 1)
    for first in range(2):
        @pl.when(is_end)
        def _():
            @pl.loop(first * pieces, (first + 1) * pieces)
            def _(block):
                filter_block(1, block)

        if first == 0:
            hand_on_peer(0)
        hand_on(1, first)
    hand_on_peer(1)

    for part in range(2):
        for turn in range(2):
            source = ctx if turn == 0 else 1 - ctx
            for half in range(2):
                hops = col if half == 0 else last - col

                @pl.when(hops > 0)
                def _():
                    z_copy(half, part, source, left).wait_recv()

                @pl.when((hops > 0) & (hops < last))
                def _():
                    z_copy(half, part, source, right if half == 0 else left).start()

    for half in range(2):
        for part in range(2):
            for source in range(2):
                place = (half * 2 + part) * 2 + source
                out_ref[:, place * width : (place + 1) * width] = gath[half, part, source]

    @pl.loop(0, pieces)
    def _(piece):
        x_copy(piece).wait_send()

    for half in range(2):
        @pl.when((last - col if half == 0 else col) < last)
        def _():
            @pl.loop(0, chunks)
            def _(chunk):
                acc_copy(half, chunk).wait_send()

        @pl.when((col if half == 0 else last - col) < last)
        def _():
            for part in range(2):
                for source in range(2):
                    z_copy(half, part, source, left).wait_send()

    @pl.when(is_end)
    def _():
        for part in range(2):
            stage_copy(part).wait_send()


def chain(last, activations, gain, weights, scale, taps):
    tokens, features = activations.shape
    rows = FILTER_LEN
    pieces = tokens // rows
    chunks = 4 * pieces
    width = weights.shape[1] // 3
    dma = pltpu.SemaphoreType.DMA
    vmem = pl.BlockSpec(memory_space=pltpu.VMEM)
    return pl.pallas_call(
        functools.partial(chain_kernel, last),
        in_specs=[vmem] * 5,
        out_specs=vmem,
        out_shape=jax.ShapeDtypeStruct((tokens, 8 * width), jnp.bfloat16),
        scratch_shapes=[
            pltpu.VMEM((2, pieces, rows, features), jnp.bfloat16),
            pltpu.VMEM((2, chunks, rows, 3 * width), jnp.bfloat16),
            pltpu.VMEM((3, SUB + rows, width), jnp.float32),
            pltpu.VMEM((SUB + rows, width), jnp.float32),
            pltpu.VMEM((SUB, 2 * rows, width), jnp.float32),
            pltpu.VMEM((2, tokens, width), jnp.bfloat16),
            pltpu.VMEM((2, 2, 2, tokens, width), jnp.bfloat16),
            dma((2, chunks)), dma((2, chunks)), dma((pieces,)), dma((pieces,)),
            dma((2,)), dma((2,)), dma((2, 2, 2)), dma((2, 2, 2)),
        ],
        compiler_params=pltpu.CompilerParams(
            collective_id=0, has_side_effects=True, vmem_limit_bytes=40 * 2**20
        ),
    )(activations, gain, weights, scale, taps)


def on_device_chain(
    n_col, activations, norm_gain, w_query, w_key, w_value, short_taps, long_taps, skip_gain, w_out
):
    ctx, col = lax.axis_index("ctx"), lax.axis_index("col")
    tokens, features = activations.shape
    held = w_query.shape[0]
    last = n_col - 1
    width = held // 4
    group = short_taps.shape[2]
    weights = jnp.stack([w_query, w_key, w_value]).reshape(3, 4, width, features)
    weights = jnp.transpose(weights, (1, 0, 2, 3)).reshape(4, 3 * width, features)

    taps = jnp.concatenate(
        [short_taps.reshape(9, group), skip_gain[None], jnp.zeros((6, group), jnp.float32), long_taps], axis=0
    )
    pairs = [(x * n_col + 2 * x + d, x * n_col + d * last) for x in range(2) for d in range(2)]
    taps = lax.ppermute(taps, ("ctx", "col"), pairs)
    taps = jnp.transpose(taps.reshape(-1, 2, width), (1, 0, 2))

    w_full = lax.all_gather(w_out, "ctx", axis=0, tiled=True)
    w_full = jnp.transpose(w_full.reshape(-1, 2, 4, width), (0, 2, 1, 3)).reshape(w_full.shape)

    as_float = activations.astype(jnp.float32)
    squares = jnp.sum(as_float * as_float, axis=1).reshape(-1, 128)
    total = squares
    for step in range(1, n_col):
        total = total + shift(squares, "col", n_col, step)
    other = shift(total, "ctx", 2, 1)
    total = jnp.where(ctx == 0, jnp.concatenate([total, other]), jnp.concatenate([other, total]))
    scale = lax.rsqrt(total / D + epsilon).reshape(-1, 1)

    block_rows = chain(last, activations, norm_gain[None], weights, scale, taps)
    out_part = lax.dot_general(
        block_rows, w_full, (((1,), (1,)), ((), ())), preferred_element_type=jnp.float32
    )
    return lax.psum_scatter(out_part.astype(jnp.bfloat16), "row", scatter_dimension=0, tiled=True)


def solution(mesh):
    in_specs = (
        P("ctx", "col"),
        P("col"),
        P(("row", "ctx"), "col"),
        P(("row", "ctx"), "col"),
        P(("row", "ctx"), "col"),
        P(None, None, ("row", "col")),
        P(None, ("row", "col")),
        P(("row", "col")),
        P(("col", "ctx"), "row"),
    )
    out_specs = P(("ctx", "row"), "col")
    n_ctx, n_row, n_col = mesh.shape["ctx"], mesh.shape["row"], mesh.shape["col"]
    if n_ctx == 2 and n_col == 4:
        body = functools.partial(on_device_chain, n_col)
    else:
        body = functools.partial(on_device, n_ctx, n_row, n_col)
    return jax.shard_map(body, mesh=mesh, in_specs=in_specs, out_specs=out_specs, check_vma=False)
```

```python
import functools

import jax
import jax.numpy as jnp
from jax import lax
from jax.experimental import pallas as pl
from jax.experimental.pallas import tpu as pltpu
from jax.sharding import PartitionSpec as P

D = 4096
SHORT_LEN = 3
FILTER_LEN = 128
SUB = 8
epsilon = 1e-05


def filter_kernel(x_ref, scale_ref, short_ref, long_ref, skip_ref, out_ref, prev, gates, shifted):
    step = pl.program_id(0)
    rows = x_ref.shape[1]

    @pl.when(step == 0)
    def _():
        prev[...] = jnp.zeros_like(prev)
        gates[0:SUB, :] = jnp.zeros((SUB, gates.shape[1]), jnp.float32)
        shifted[:, 0:FILTER_LEN, :] = jnp.zeros((SUB, FILTER_LEN, shifted.shape[2]), jnp.float32)

    @pl.when(step > 0)
    def _():
        shifted[:, 0:FILTER_LEN, :] = shifted[:, rows : rows + FILTER_LEN, :]

    filtered = []
    for which in range(3):
        now = x_ref[which].astype(jnp.float32) * scale_ref[...]
        prev[which, SUB:, :] = now
        total = short_ref[which, 0:1, :] * now
        for tap in range(1, SHORT_LEN):
            total = total + short_ref[which, tap : tap + 1, :] * prev[which, SUB - tap : SUB - tap + rows, :]
        filtered.append(total)
        prev[which, 0:SUB, :] = prev[which, rows : rows + SUB, :]
    gate = filtered[1] * filtered[2]
    gates[SUB:, :] = gate
    for move in range(SUB):
        shifted[move, FILTER_LEN:, :] = gates[SUB - move : SUB - move + rows, :]
    gates[0:SUB, :] = gates[rows : rows + SUB, :]
    total = skip_ref[...] * gate
    for move in range(SUB):
        for back in range(0, FILTER_LEN, SUB):
            total = total + long_ref[back + move : back + move + 1, :] * shifted[
                move, FILTER_LEN - back : FILTER_LEN - back + rows, :
            ]
    out_ref[...] = (filtered[0] * total).astype(out_ref.dtype)


def mix(stacked, scale, short_taps, long_taps, skip_gain):
    _, tokens, channels = stacked.shape
    rows = FILTER_LEN
    return pl.pallas_call(
        filter_kernel,
        grid=(tokens // rows,),
        in_specs=[
            pl.BlockSpec((3, rows, channels), lambda i: (0, i, 0)),
            pl.BlockSpec((rows, 1), lambda i: (i, 0)),
            pl.BlockSpec((3, SHORT_LEN, channels), lambda i: (0, 0, 0)),
            pl.BlockSpec((FILTER_LEN, channels), lambda i: (0, 0)),
            pl.BlockSpec((1, channels), lambda i: (0, 0)),
        ],
        out_specs=pl.BlockSpec((rows, channels), lambda i: (i, 0)),
        out_shape=jax.ShapeDtypeStruct((tokens, channels), jnp.bfloat16),
        scratch_shapes=[
            pltpu.VMEM((3, SUB + rows, channels), jnp.float32),
            pltpu.VMEM((SUB + rows, channels), jnp.float32),
            pltpu.VMEM((SUB, FILTER_LEN + rows, channels), jnp.float32),
        ],
    )(stacked, scale, short_taps, long_taps, skip_gain)


def shift(value, axis, size, by):
    return lax.ppermute(value, axis, [((i + by) % size, i) for i in range(size)])


def on_device(
    n_ctx, n_row, n_col,
    activations, norm_gain, w_query, w_key, w_value, short_taps, long_taps, skip_gain, w_out,
):
    ctx, col = lax.axis_index("ctx"), lax.axis_index("col")
    tokens, features = activations.shape
    held = w_query.shape[0]
    width = held // n_col
    stacked = jnp.stack([w_query, w_key, w_value]).reshape(3, n_col, width, features)

    taps = jnp.concatenate([short_taps.reshape(9, -1), long_taps, skip_gain[None]], axis=0)
    taps = lax.all_gather(taps, "col", axis=1, tiled=True)
    taps = lax.dynamic_slice_in_dim(taps, ctx * held + col * width, width, 1)

    w_full = lax.all_gather(w_out, "ctx", axis=0, tiled=True)
    w_full = jnp.transpose(w_full.reshape(-1, n_ctx, n_col, width), (0, 2, 1, 3)).reshape(w_full.shape)

    qkv = jnp.zeros((3, n_ctx * tokens, width), jnp.bfloat16)
    squares = jnp.zeros((n_ctx * tokens,), jnp.float32)
    for step in range(n_ctx):
        part = activations if step == 0 else shift(activations, "ctx", n_ctx, step)
        first = lax.rem(ctx + step, n_ctx) * tokens
        as_float = part.astype(jnp.float32)
        squares = lax.dynamic_update_slice(squares, jnp.sum(as_float * as_float, axis=1), (first,))
        scaled = (as_float * norm_gain).astype(jnp.bfloat16)
        partial_value = jnp.einsum("td,skcd->kstc", scaled, stacked, preferred_element_type=jnp.float32)
        summed = lax.psum_scatter(partial_value.astype(jnp.bfloat16), "col", scatter_dimension=0, tiled=True)
        qkv = lax.dynamic_update_slice(qkv, summed[0], (0, first, 0))

    total = squares.reshape(-1, 128)
    for step in range(1, n_col):
        total = total + shift(squares.reshape(-1, 128), "col", n_col, step)
    scale = lax.rsqrt(total / D + epsilon).reshape(-1, 1)

    mixed = mix(qkv, scale, taps[:9].reshape(3, 3, width), taps[9:-1], taps[-1:])

    spread = lax.all_to_all(
        mixed.reshape(n_ctx, tokens, width), "ctx", split_axis=0, concat_axis=0, tiled=True
    )
    spread = jnp.transpose(spread, (1, 0, 2)).reshape(tokens, n_ctx * width)
    block_rows = lax.all_gather(spread, "col", axis=1, tiled=True)
    out_part = lax.dot_general(
        block_rows, w_full, (((1,), (1,)), ((), ())), preferred_element_type=jnp.float32
    )
    return lax.psum_scatter(out_part.astype(jnp.bfloat16), "row", scatter_dimension=0, tiled=True)


QUARTERS = 4


def chain_kernel(
    last, x_ref, gain_ref, wq_ref, wk_ref, wv_ref, squares_ref, own_taps, out_ref,
    xs, w_ref, acc, taps_ref, totals, prev, gates, shifted, stage, gath,
    w_sem, taps_send, taps_recv, sq_send, sq_recv,
    acc_send, acc_recv, x_send, x_recv, stage_send, stage_recv, z_send, z_recv,
):
    ctx, col = lax.axis_index("ctx"), lax.axis_index("col")
    pieces = xs.shape[1]
    chunks = acc.shape[1]
    rows = xs.shape[2]
    width = gath.shape[4]
    quarter = gath.shape[3] // QUARTERS
    per = pieces // QUARTERS
    n_col = last + 1
    is_end = (col == 0) | (col == last)
    end_half = jnp.where(col == 0, 0, 1)
    left, right = jnp.maximum(col - 1, 0), jnp.minimum(col + 1, last)
    peer = {"ctx": 1 - ctx}
    mesh_ids = pl.DeviceIdType.MESH

    def w_copy(group, which):
        source = (wq_ref, wk_ref, wv_ref)[which]
        return pltpu.make_async_copy(
            source.at[pl.ds(group * width, width)], w_ref.at[group, pl.ds(which * width, width)],
            w_sem.at[group, which],
        )

    for group in range(4):
        for which in range(3):
            w_copy(group, which).start()

    barrier = pltpu.get_barrier_semaphore()
    for far in range(2):
        for away in range(n_col):
            if far or away:
                other = {"ctx": lax.rem(ctx + far, 2), "col": lax.rem(col + away, n_col)}
                pl.semaphore_signal(barrier, inc=1, device_id=other, device_id_type=mesh_ids)

    xs[0] = (x_ref[...].astype(jnp.float32) * gain_ref[...]).astype(jnp.bfloat16).reshape(xs.shape[1:])
    pl.semaphore_wait(barrier, 2 * n_col - 1)

    def x_copy(piece):
        return pltpu.make_async_remote_copy(
            xs.at[0, piece], xs.at[1, piece], x_send.at[piece], x_recv.at[piece],
            device_id=peer, device_id_type=mesh_ids,
        )

    def acc_copy(half, chunk):
        return pltpu.make_async_remote_copy(
            acc.at[half, chunk], acc.at[half, chunk], acc_send.at[half, chunk], acc_recv.at[half, chunk],
            device_id={"col": left if half == 0 else right}, device_id_type=mesh_ids,
        )

    def stage_copy(part, place):
        rows_of = pl.ds(pl.multiple_of(place * quarter, quarter), quarter)
        return pltpu.make_async_remote_copy(
            stage.at[part, rows_of], gath.at[end_half, part, ctx, rows_of],
            stage_send.at[part, place], stage_recv.at[part, place],
            device_id=peer, device_id_type=mesh_ids,
        )

    def z_copy(half, part, source, place):
        rows_of = pl.ds(pl.multiple_of(place * quarter, quarter), quarter)
        return pltpu.make_async_remote_copy(
            gath.at[half, part, source, rows_of], gath.at[half, part, source, rows_of],
            z_send.at[half, part, source, place], z_recv.at[half, part, source, place],
            device_id={"col": right if half == 0 else left}, device_id_type=mesh_ids,
        )

    def sq_copy(far, away):
        me = ctx * n_col + col
        return pltpu.make_async_remote_copy(
            squares_ref, totals.at[me], sq_send.at[far, 0 if away == 0 else 1], sq_recv.at[me],
            device_id={"ctx": lax.rem(ctx + far, 2), "col": away}, device_id_type=mesh_ids,
        )

    taps_owner = col // 2 == ctx
    taps_end = lax.rem(col, 2) * last
    taps_copy = pltpu.make_async_remote_copy(
        own_taps, taps_ref, taps_send, taps_recv, device_id={"col": taps_end}, device_id_type=mesh_ids
    )

    @pl.loop(0, pieces)
    def _(piece):
        x_copy(piece).start()

    for far in range(2):
        for away in (0, last):
            @pl.when((col != away) if far == 0 else (col >= 0))
            def _():
                sq_copy(far, away).start()

    @pl.when(taps_owner & (taps_end != col))
    def _():
        taps_copy.start()

    @pl.when(taps_owner & (taps_end == col))
    def _():
        taps_ref[...] = own_taps[...]

    @pl.when(is_end)
    def _():
        totals[ctx * n_col + col] = squares_ref[...]

    for group in range(4):
        for which in range(3):
            w_copy(group, which).wait()

    def wait_small():
        for source in range(2 * n_col):
            @pl.when(source != ctx * n_col + col)
            def _():
                pltpu.make_async_remote_copy(
                    squares_ref, totals.at[source], sq_send.at[0, 0], sq_recv.at[source],
                    device_id=peer, device_id_type=mesh_ids,
                ).wait_recv()

        @pl.when(jnp.logical_not(taps_owner & (taps_end == col)))
        def _():
            taps_copy.wait_recv()

        for half in range(2):
            total = totals[half * n_col]
            for source in range(1, n_col):
                total = total + totals[half * n_col + source]
            totals[half * n_col] = lax.rsqrt(total / D + epsilon)

    diagonal = lax.broadcasted_iota(jnp.int32, (rows, rows), 0) == lax.broadcasted_iota(
        jnp.int32, (rows, rows), 1
    )

    def filter_block(part, mine, place, again):
        chunk = mine * 2 * pieces + part * pieces + place
        half = lax.rem(ctx + mine, 2)
        row_scale = totals[half * n_col, pl.ds(place, 1), :]
        scale = jnp.sum(jnp.where(diagonal, row_scale, 0.0), axis=1, keepdims=True)
        taps = taps_ref.at[part]

        if not again:
            @pl.when((place == 0) & ((mine == 0) | (ctx == 1)))
            def _():
                prev[part] = jnp.zeros(prev.shape[1:], jnp.float32)
                gates[part, 0:SUB, :] = jnp.zeros((SUB, width), jnp.float32)
                shifted[part, :, rows:, :] = jnp.zeros((SUB, rows, width), jnp.float32)

        shifted[part, :, 0:rows, :] = shifted[part, :, rows:, :]
        filtered = []
        for which in range(3):
            now = acc[end_half, chunk, :, which * width : (which + 1) * width].astype(jnp.float32) * scale
            prev[part, which, SUB:, :] = now
            total = taps[3 * which : 3 * which + 1, :] * now
            for tap in range(1, SHORT_LEN):
                row = 3 * which + tap
                total = total + taps[row : row + 1, :] * prev[part, which, SUB - tap : SUB - tap + rows, :]
            filtered.append(total)
            prev[part, which, 0:SUB, :] = prev[part, which, rows : rows + SUB, :]
        gate = filtered[1] * filtered[2]
        gates[part, SUB:, :] = gate
        for move in range(SUB):
            shifted[part, move, rows:, :] = gates[part, SUB - move : SUB - move + rows, :]
        gates[part, 0:SUB, :] = gates[part, rows : rows + SUB, :]
        total = taps[9:10, :] * gate
        for move in range(SUB):
            for back in range(0, FILTER_LEN, SUB):
                row = 16 + back + move
                total = total + taps[row : row + 1, :] * shifted[part, move, rows - back : 2 * rows - back, :]
        value = (filtered[0] * total).astype(jnp.bfloat16)
        spot = pl.ds(pl.multiple_of(place * rows, rows), rows)

        @pl.when(mine == 0)
        def _():
            gath[end_half, part, ctx, spot, :] = value

        @pl.when(mine == 1)
        def _():
            stage[part, spot, :] = value

    def pass_on(half, hops, part, source, place, from_peer):
        @pl.when(hops > 0)
        def _():
            z_copy(half, part, source, place).wait_recv()

        if from_peer:
            @pl.when(hops == 0)
            def _():
                stage_copy(part, place).wait_recv()

        @pl.when(hops < last)
        def _():
            z_copy(half, part, source, place).start()

    @pl.loop(0, chunks + 4 * last)
    def _(step):
        first = step - 2 * jnp.minimum(col, last - col)

        @pl.when((first >= 2 * pieces) & (first < 3 * pieces))
        def _():
            x_copy(first - 2 * pieces).wait_recv()

        for half in range(2):
            hops = last - col if half == 0 else col
            chunk = step - 2 * hops

            @pl.when((chunk >= 0) & (chunk < chunks))
            def _():
                part = lax.rem(chunk // pieces, 2)
                own = lax.dot_general(
                    xs[chunk // (2 * pieces), lax.rem(chunk, pieces)], w_ref[2 * half + part],
                    (((1,), (1,)), ((), ())), preferred_element_type=jnp.float32,
                )

                @pl.when(hops == 0)
                def _():
                    acc[half, chunk] = own.astype(jnp.bfloat16)

                @pl.when(hops > 0)
                def _():
                    acc_copy(half, chunk).wait_recv()
                    acc[half, chunk] = (own + acc[half, chunk].astype(jnp.float32)).astype(jnp.bfloat16)

                @pl.when(hops < last)
                def _():
                    acc_copy(half, chunk).start()

        done = step - 2 * last

        @pl.when(is_end & (done == 0))
        def _():
            wait_small()

        @pl.when(is_end & (done >= 0) & (done < chunks))
        def _():
            mine, part, place = done // (2 * pieces), lax.rem(done // pieces, 2), lax.rem(done, pieces)
            filter_block(part, mine, place, False)

            @pl.when((mine == 1) & (lax.rem(place, per) == per - 1))
            def _():
                stage_copy(part, place // per).start()

            @pl.when((mine == 1) & (place == pieces - 1) & (ctx == 1))
            def _():
                filter_block(part, 0, 0, True)

        for half in range(2):
            hops = col if half == 0 else last - col
            event = step - 2 * last - 2 * hops
            full = lax.rem(event + per, per) == per - 1
            index = event // per

            @pl.when((event >= 0) & (event < 2 * pieces) & full)
            def _():
                place = lax.rem(index, QUARTERS)

                @pl.when((ctx == 0) | (place > 0))
                def _():
                    pass_on(half, hops, index // QUARTERS, ctx, place, False)

            @pl.when((event >= 2 * pieces + per) & (event < chunks) & full)
            def _():
                late = index - 2 * QUARTERS - 1
                pass_on(half, hops, late // QUARTERS, 1 - ctx, lax.rem(late, QUARTERS), True)

            @pl.when((event == 3 * pieces) & (ctx == 1))
            def _():
                pass_on(half, hops, 0, ctx, 0, False)

    for half in range(2):
        hops = col if half == 0 else last - col
        @pl.when(ctx == 1)
        def _():
            pass_on(half, hops, 1, ctx, 0, False)

        pass_on(half, hops, 1, 1 - ctx, QUARTERS - 1, True)

    for half in range(2):
        for part in range(2):
            for source in range(2):
                place = (half * 2 + part) * 2 + source
                out_ref[:, place * width : (place + 1) * width] = gath[half, part, source]

    @pl.loop(0, pieces)
    def _(piece):
        x_copy(piece).wait_send()

    for far in range(2):
        for away in (0, last):
            @pl.when((col != away) if far == 0 else (col >= 0))
            def _():
                sq_copy(far, away).wait_send()

    @pl.when(taps_owner & (taps_end != col))
    def _():
        taps_copy.wait_send()

    for half in range(2):
        @pl.when((last - col if half == 0 else col) < last)
        def _():
            @pl.loop(0, chunks)
            def _(chunk):
                acc_copy(half, chunk).wait_send()

        @pl.when((col if half == 0 else last - col) < last)
        def _():
            for part in range(2):
                for source in range(2):
                    for place in range(QUARTERS):
                        z_copy(half, part, source, place).wait_send()

    @pl.when(is_end)
    def _():
        for part in range(2):
            for place in range(QUARTERS):
                stage_copy(part, place).wait_send()


def chain(last, activations, gain, weights, squares, taps):
    tokens, features = activations.shape
    rows = FILTER_LEN
    pieces = tokens // rows
    chunks = 4 * pieces
    width = weights[0].shape[0] // 4
    dma = pltpu.SemaphoreType.DMA
    vmem = pl.BlockSpec(memory_space=pltpu.VMEM)
    hbm = pl.BlockSpec(memory_space=pl.ANY)
    return pl.pallas_call(
        functools.partial(chain_kernel, last),
        in_specs=[vmem, vmem, hbm, hbm, hbm, vmem, vmem],
        out_specs=vmem,
        out_shape=jax.ShapeDtypeStruct((tokens, 8 * width), jnp.bfloat16),
        scratch_shapes=[
            pltpu.VMEM((2, pieces, rows, features), jnp.bfloat16),
            pltpu.VMEM((4, 3 * width, features), jnp.bfloat16),
            pltpu.VMEM((2, chunks, rows, 3 * width), jnp.bfloat16),
            pltpu.VMEM(taps.shape, jnp.float32),
            pltpu.VMEM((2 * (last + 1),) + squares.shape, jnp.float32),
            pltpu.VMEM((2, 3, SUB + rows, width), jnp.float32),
            pltpu.VMEM((2, SUB + rows, width), jnp.float32),
            pltpu.VMEM((2, SUB, 2 * rows, width), jnp.float32),
            pltpu.VMEM((2, tokens, width), jnp.bfloat16),
            pltpu.VMEM((2, 2, 2, tokens, width), jnp.bfloat16),
            dma((4, 3)), dma, dma, dma((2, 2)), dma((2 * (last + 1),)),
            dma((2, chunks)), dma((2, chunks)), dma((pieces,)), dma((pieces,)),
            dma((2, QUARTERS)), dma((2, QUARTERS)), dma((2, 2, 2, QUARTERS)), dma((2, 2, 2, QUARTERS)),
        ],
        compiler_params=pltpu.CompilerParams(
            collective_id=0, has_side_effects=True, vmem_limit_bytes=44 * 2**20
        ),
    )(activations, gain, *weights, squares, taps)


def on_device_chain(
    n_col, activations, norm_gain, w_query, w_key, w_value, short_taps, long_taps, skip_gain, w_out
):
    held = w_query.shape[0]
    width = held // 4
    group = short_taps.shape[2]

    taps = jnp.concatenate(
        [short_taps.reshape(9, group), skip_gain[None], jnp.zeros((6, group), jnp.float32), long_taps], axis=0
    )
    taps = jnp.transpose(taps.reshape(-1, 2, width), (1, 0, 2))

    w_full = lax.all_gather(w_out, "ctx", axis=0, tiled=True)
    w_full = jnp.transpose(w_full.reshape(-1, 2, 4, width), (0, 2, 1, 3)).reshape(w_full.shape)

    as_float = activations.astype(jnp.float32)
    squares = jnp.sum(as_float * as_float, axis=1).reshape(-1, FILTER_LEN)

    block_rows = chain(n_col - 1, activations, norm_gain[None], (w_query, w_key, w_value), squares, taps)
    out_part = lax.dot_general(
        block_rows, w_full, (((1,), (1,)), ((), ())), preferred_element_type=jnp.float32
    )
    return lax.psum_scatter(out_part.astype(jnp.bfloat16), "row", scatter_dimension=0, tiled=True)


def solution(mesh):
    in_specs = (
        P("ctx", "col"),
        P("col"),
        P(("row", "ctx"), "col"),
        P(("row", "ctx"), "col"),
        P(("row", "ctx"), "col"),
        P(None, None, ("row", "col")),
        P(None, ("row", "col")),
        P(("row", "col")),
        P(("col", "ctx"), "row"),
    )
    out_specs = P(("ctx", "row"), "col")
    n_ctx, n_row, n_col = mesh.shape["ctx"], mesh.shape["row"], mesh.shape["col"]
    if n_ctx == 2 and n_col == 4:
        body = functools.partial(on_device_chain, n_col)
    else:
        body = functools.partial(on_device, n_ctx, n_row, n_col)
    return jax.shard_map(body, mesh=mesh, in_specs=in_specs, out_specs=out_specs, check_vma=False)
```

```python
import functools

import jax
import jax.numpy as jnp
from jax import lax
from jax.experimental import pallas as pl
from jax.experimental.pallas import tpu as pltpu
from jax.sharding import PartitionSpec as P

D = 4096
SHORT_LEN = 3
FILTER_LEN = 128
SUB = 8
epsilon = 1e-05


def filter_kernel(x_ref, scale_ref, short_ref, long_ref, skip_ref, out_ref, prev, gates, shifted):
    step = pl.program_id(0)
    rows = x_ref.shape[1]

    @pl.when(step == 0)
    def _():
        prev[...] = jnp.zeros_like(prev)
        gates[0:SUB, :] = jnp.zeros((SUB, gates.shape[1]), jnp.float32)
        shifted[:, 0:FILTER_LEN, :] = jnp.zeros((SUB, FILTER_LEN, shifted.shape[2]), jnp.float32)

    @pl.when(step > 0)
    def _():
        shifted[:, 0:FILTER_LEN, :] = shifted[:, rows : rows + FILTER_LEN, :]

    filtered = []
    for which in range(3):
        now = x_ref[which].astype(jnp.float32) * scale_ref[...]
        prev[which, SUB:, :] = now
        total = short_ref[which, 0:1, :] * now
        for tap in range(1, SHORT_LEN):
            total = total + short_ref[which, tap : tap + 1, :] * prev[which, SUB - tap : SUB - tap + rows, :]
        filtered.append(total)
        prev[which, 0:SUB, :] = prev[which, rows : rows + SUB, :]
    gate = filtered[1] * filtered[2]
    gates[SUB:, :] = gate
    for move in range(SUB):
        shifted[move, FILTER_LEN:, :] = gates[SUB - move : SUB - move + rows, :]
    gates[0:SUB, :] = gates[rows : rows + SUB, :]
    total = skip_ref[...] * gate
    for move in range(SUB):
        for back in range(0, FILTER_LEN, SUB):
            total = total + long_ref[back + move : back + move + 1, :] * shifted[
                move, FILTER_LEN - back : FILTER_LEN - back + rows, :
            ]
    out_ref[...] = (filtered[0] * total).astype(out_ref.dtype)


def mix(stacked, scale, short_taps, long_taps, skip_gain):
    _, tokens, channels = stacked.shape
    rows = FILTER_LEN
    return pl.pallas_call(
        filter_kernel,
        grid=(tokens // rows,),
        in_specs=[
            pl.BlockSpec((3, rows, channels), lambda i: (0, i, 0)),
            pl.BlockSpec((rows, 1), lambda i: (i, 0)),
            pl.BlockSpec((3, SHORT_LEN, channels), lambda i: (0, 0, 0)),
            pl.BlockSpec((FILTER_LEN, channels), lambda i: (0, 0)),
            pl.BlockSpec((1, channels), lambda i: (0, 0)),
        ],
        out_specs=pl.BlockSpec((rows, channels), lambda i: (i, 0)),
        out_shape=jax.ShapeDtypeStruct((tokens, channels), jnp.bfloat16),
        scratch_shapes=[
            pltpu.VMEM((3, SUB + rows, channels), jnp.float32),
            pltpu.VMEM((SUB + rows, channels), jnp.float32),
            pltpu.VMEM((SUB, FILTER_LEN + rows, channels), jnp.float32),
        ],
    )(stacked, scale, short_taps, long_taps, skip_gain)


def shift(value, axis, size, by):
    return lax.ppermute(value, axis, [((i + by) % size, i) for i in range(size)])


def on_device(
    n_ctx, n_row, n_col,
    activations, norm_gain, w_query, w_key, w_value, short_taps, long_taps, skip_gain, w_out,
):
    ctx, col = lax.axis_index("ctx"), lax.axis_index("col")
    tokens, features = activations.shape
    held = w_query.shape[0]
    width = held // n_col
    stacked = jnp.stack([w_query, w_key, w_value]).reshape(3, n_col, width, features)

    taps = jnp.concatenate([short_taps.reshape(9, -1), long_taps, skip_gain[None]], axis=0)
    taps = lax.all_gather(taps, "col", axis=1, tiled=True)
    taps = lax.dynamic_slice_in_dim(taps, ctx * held + col * width, width, 1)

    w_full = lax.all_gather(w_out, "ctx", axis=0, tiled=True)
    w_full = jnp.transpose(w_full.reshape(-1, n_ctx, n_col, width), (0, 2, 1, 3)).reshape(w_full.shape)

    qkv = jnp.zeros((3, n_ctx * tokens, width), jnp.bfloat16)
    squares = jnp.zeros((n_ctx * tokens,), jnp.float32)
    for step in range(n_ctx):
        part = activations if step == 0 else shift(activations, "ctx", n_ctx, step)
        first = lax.rem(ctx + step, n_ctx) * tokens
        as_float = part.astype(jnp.float32)
        squares = lax.dynamic_update_slice(squares, jnp.sum(as_float * as_float, axis=1), (first,))
        scaled = (as_float * norm_gain).astype(jnp.bfloat16)
        partial_value = jnp.einsum("td,skcd->kstc", scaled, stacked, preferred_element_type=jnp.float32)
        summed = lax.psum_scatter(partial_value.astype(jnp.bfloat16), "col", scatter_dimension=0, tiled=True)
        qkv = lax.dynamic_update_slice(qkv, summed[0], (0, first, 0))

    total = squares.reshape(-1, 128)
    for step in range(1, n_col):
        total = total + shift(squares.reshape(-1, 128), "col", n_col, step)
    scale = lax.rsqrt(total / D + epsilon).reshape(-1, 1)

    mixed = mix(qkv, scale, taps[:9].reshape(3, 3, width), taps[9:-1], taps[-1:])

    spread = lax.all_to_all(
        mixed.reshape(n_ctx, tokens, width), "ctx", split_axis=0, concat_axis=0, tiled=True
    )
    spread = jnp.transpose(spread, (1, 0, 2)).reshape(tokens, n_ctx * width)
    block_rows = lax.all_gather(spread, "col", axis=1, tiled=True)
    out_part = lax.dot_general(
        block_rows, w_full, (((1,), (1,)), ((), ())), preferred_element_type=jnp.float32
    )
    return lax.psum_scatter(out_part.astype(jnp.bfloat16), "row", scatter_dimension=0, tiled=True)


QUARTERS = 4


def chain_kernel(
    last, x_ref, gain_ref, wq_ref, wk_ref, wv_ref, squares_ref, own_taps, out_ref,
    xs, w_rows, w_ref, acc, taps_ref, totals, prev, gates, shifted, stage, gath,
    w_sem, taps_send, taps_recv, sq_send, sq_recv,
    acc_send, acc_recv, x_send, x_recv, stage_send, stage_recv, z_send, z_recv,
):
    ctx, col = lax.axis_index("ctx"), lax.axis_index("col")
    pieces = xs.shape[1]
    chunks = acc.shape[1]
    rows = xs.shape[2]
    width = gath.shape[4]
    quarter = gath.shape[3] // QUARTERS
    per = pieces // QUARTERS
    n_col = last + 1
    is_end = (col == 0) | (col == last)
    end_half = jnp.where(col == 0, 0, 1)
    left, right = jnp.maximum(col - 1, 0), jnp.minimum(col + 1, last)
    peer = {"ctx": 1 - ctx}
    mesh_ids = pl.DeviceIdType.MESH

    def w_copy(group, which):
        source = (wq_ref, wk_ref, wv_ref)[which]
        return pltpu.make_async_copy(
            source.at[pl.ds(group * width, width)], w_rows.at[group, pl.ds(which * width, width)],
            w_sem.at[group, which],
        )

    for group in range(4):
        for which in range(3):
            w_copy(group, which).start()

    barrier = pltpu.get_barrier_semaphore()
    for far in range(2):
        for away in range(n_col):
            if far or away:
                other = {"ctx": lax.rem(ctx + far, 2), "col": lax.rem(col + away, n_col)}
                pl.semaphore_signal(barrier, inc=1, device_id=other, device_id_type=mesh_ids)

    xs[0] = (x_ref[...].astype(jnp.float32) * gain_ref[...]).astype(jnp.bfloat16).reshape(xs.shape[1:])
    pl.semaphore_wait(barrier, 2 * n_col - 1)

    def x_copy(piece):
        return pltpu.make_async_remote_copy(
            xs.at[0, piece], xs.at[1, piece], x_send.at[piece], x_recv.at[piece],
            device_id=peer, device_id_type=mesh_ids,
        )

    def acc_copy(half, chunk):
        return pltpu.make_async_remote_copy(
            acc.at[half, chunk], acc.at[half, chunk], acc_send.at[half, chunk], acc_recv.at[half, chunk],
            device_id={"col": left if half == 0 else right}, device_id_type=mesh_ids,
        )

    def stage_copy(part, place):
        rows_of = pl.ds(pl.multiple_of(place * quarter, quarter), quarter)
        return pltpu.make_async_remote_copy(
            stage.at[part, rows_of], gath.at[end_half, part, ctx, rows_of],
            stage_send.at[part, place], stage_recv.at[part, place],
            device_id=peer, device_id_type=mesh_ids,
        )

    def z_copy(half, part, source, place):
        rows_of = pl.ds(pl.multiple_of(place * quarter, quarter), quarter)
        return pltpu.make_async_remote_copy(
            gath.at[half, part, source, rows_of], gath.at[half, part, source, rows_of],
            z_send.at[half, part, source, place], z_recv.at[half, part, source, place],
            device_id={"col": right if half == 0 else left}, device_id_type=mesh_ids,
        )

    def sq_copy(far, away):
        me = ctx * n_col + col
        return pltpu.make_async_remote_copy(
            squares_ref, totals.at[me], sq_send.at[far, 0 if away == 0 else 1], sq_recv.at[me],
            device_id={"ctx": lax.rem(ctx + far, 2), "col": away}, device_id_type=mesh_ids,
        )

    taps_owner = col // 2 == ctx
    taps_end = lax.rem(col, 2) * last
    taps_copy = pltpu.make_async_remote_copy(
        own_taps, taps_ref, taps_send, taps_recv, device_id={"col": taps_end}, device_id_type=mesh_ids
    )

    @pl.loop(0, pieces)
    def _(piece):
        x_copy(piece).start()

    for far in range(2):
        for away in (0, last):
            @pl.when((col != away) if far == 0 else (col >= 0))
            def _():
                sq_copy(far, away).start()

    @pl.when(taps_owner & (taps_end != col))
    def _():
        taps_copy.start()

    @pl.when(taps_owner & (taps_end == col))
    def _():
        taps_ref[...] = own_taps[...]

    @pl.when(is_end)
    def _():
        totals[ctx * n_col + col] = squares_ref[...]

    for group in range(4):
        for which in range(3):
            w_copy(group, which).wait()

    @pl.loop(0, 4)
    def _(group):
        w_ref[group] = jnp.transpose(w_rows[group])

    def wait_small():
        for source in range(2 * n_col):
            @pl.when(source != ctx * n_col + col)
            def _():
                pltpu.make_async_remote_copy(
                    squares_ref, totals.at[source], sq_send.at[0, 0], sq_recv.at[source],
                    device_id=peer, device_id_type=mesh_ids,
                ).wait_recv()

        @pl.when(jnp.logical_not(taps_owner & (taps_end == col)))
        def _():
            taps_copy.wait_recv()

        for half in range(2):
            total = totals[half * n_col]
            for source in range(1, n_col):
                total = total + totals[half * n_col + source]
            totals[half * n_col] = lax.rsqrt(total / D + epsilon)

    diagonal = lax.broadcasted_iota(jnp.int32, (rows, rows), 0) == lax.broadcasted_iota(
        jnp.int32, (rows, rows), 1
    )

    def filter_block(part, mine, place, again):
        chunk = mine * 2 * pieces + part * pieces + place
        half = lax.rem(ctx + mine, 2)
        row_scale = totals[half * n_col, pl.ds(place, 1), :]
        scale = jnp.sum(jnp.where(diagonal, row_scale, 0.0), axis=1, keepdims=True)
        taps = taps_ref.at[part]

        if not again:
            @pl.when((place == 0) & ((mine == 0) | (ctx == 1)))
            def _():
                prev[part] = jnp.zeros(prev.shape[1:], jnp.float32)
                gates[part, 0:SUB, :] = jnp.zeros((SUB, width), jnp.float32)
                shifted[part, :, rows:, :] = jnp.zeros((SUB, rows, width), jnp.float32)

        shifted[part, :, 0:rows, :] = shifted[part, :, rows:, :]
        filtered = []
        for which in range(3):
            now = acc[end_half, chunk, :, which * width : (which + 1) * width].astype(jnp.float32) * scale
            prev[part, which, SUB:, :] = now
            total = taps[3 * which : 3 * which + 1, :] * now
            for tap in range(1, SHORT_LEN):
                row = 3 * which + tap
                total = total + taps[row : row + 1, :] * prev[part, which, SUB - tap : SUB - tap + rows, :]
            filtered.append(total)
            prev[part, which, 0:SUB, :] = prev[part, which, rows : rows + SUB, :]
        gate = filtered[1] * filtered[2]
        gates[part, SUB:, :] = gate
        for move in range(SUB):
            shifted[part, move, rows:, :] = gates[part, SUB - move : SUB - move + rows, :]
        gates[part, 0:SUB, :] = gates[part, rows : rows + SUB, :]
        total = taps[9:10, :] * gate
        for move in range(SUB):
            window = shifted[part, move]
            for back in range(0, FILTER_LEN, SUB):
                row = 16 + back + move
                total = total + taps[row : row + 1, :] * window[rows - back : 2 * rows - back, :]
        value = (filtered[0] * total).astype(jnp.bfloat16)
        spot = pl.ds(pl.multiple_of(place * rows, rows), rows)

        @pl.when(mine == 0)
        def _():
            gath[end_half, part, ctx, spot, :] = value

        @pl.when(mine == 1)
        def _():
            stage[part, spot, :] = value

    def pass_on(half, hops, part, source, place, from_peer):
        @pl.when(hops > 0)
        def _():
            z_copy(half, part, source, place).wait_recv()

        if from_peer:
            @pl.when(hops == 0)
            def _():
                stage_copy(part, place).wait_recv()

        @pl.when(hops < last)
        def _():
            z_copy(half, part, source, place).start()

    @pl.loop(0, chunks + 4 * last)
    def _(step):
        first = step - 2 * jnp.minimum(col, last - col)

        @pl.when((first >= 2 * pieces) & (first < 3 * pieces))
        def _():
            x_copy(first - 2 * pieces).wait_recv()

        for half in range(2):
            hops = last - col if half == 0 else col
            chunk = step - 2 * hops

            @pl.when((chunk >= 0) & (chunk < chunks))
            def _():
                part = lax.rem(chunk // pieces, 2)
                own = lax.dot_general(
                    xs[chunk // (2 * pieces), lax.rem(chunk, pieces)], w_ref[2 * half + part],
                    (((1,), (0,)), ((), ())), preferred_element_type=jnp.float32,
                )

                @pl.when(hops == 0)
                def _():
                    acc[half, chunk] = own.astype(jnp.bfloat16)

                @pl.when(hops > 0)
                def _():
                    acc_copy(half, chunk).wait_recv()
                    acc[half, chunk] = (own + acc[half, chunk].astype(jnp.float32)).astype(jnp.bfloat16)

                @pl.when(hops < last)
                def _():
                    acc_copy(half, chunk).start()

        done = step - 2 * last

        @pl.when(is_end & (done == 0))
        def _():
            wait_small()

        @pl.when(is_end & (done >= 0) & (done < chunks))
        def _():
            mine, part, place = done // (2 * pieces), lax.rem(done // pieces, 2), lax.rem(done, pieces)
            filter_block(part, mine, place, False)

            @pl.when((mine == 1) & (lax.rem(place, per) == per - 1))
            def _():
                stage_copy(part, place // per).start()

            @pl.when((mine == 1) & (place == pieces - 1) & (ctx == 1))
            def _():
                filter_block(part, 0, 0, True)

        for half in range(2):
            hops = col if half == 0 else last - col
            event = step - 2 * last - 2 * hops
            full = lax.rem(event + per, per) == per - 1
            index = event // per

            @pl.when((event >= 0) & (event < 2 * pieces) & full)
            def _():
                place = lax.rem(index, QUARTERS)

                @pl.when((ctx == 0) | (place > 0))
                def _():
                    pass_on(half, hops, index // QUARTERS, ctx, place, False)

            @pl.when((event >= 2 * pieces + per) & (event < chunks) & full)
            def _():
                late = index - 2 * QUARTERS - 1
                pass_on(half, hops, late // QUARTERS, 1 - ctx, lax.rem(late, QUARTERS), True)

            @pl.when((event == 3 * pieces) & (ctx == 1))
            def _():
                pass_on(half, hops, 0, ctx, 0, False)

    for half in range(2):
        hops = col if half == 0 else last - col
        @pl.when(ctx == 1)
        def _():
            pass_on(half, hops, 1, ctx, 0, False)

        pass_on(half, hops, 1, 1 - ctx, QUARTERS - 1, True)

    for half in range(2):
        for part in range(2):
            for source in range(2):
                place = (half * 2 + part) * 2 + source
                out_ref[:, place * width : (place + 1) * width] = gath[half, part, source]

    @pl.loop(0, pieces)
    def _(piece):
        x_copy(piece).wait_send()

    for far in range(2):
        for away in (0, last):
            @pl.when((col != away) if far == 0 else (col >= 0))
            def _():
                sq_copy(far, away).wait_send()

    @pl.when(taps_owner & (taps_end != col))
    def _():
        taps_copy.wait_send()

    for half in range(2):
        @pl.when((last - col if half == 0 else col) < last)
        def _():
            @pl.loop(0, chunks)
            def _(chunk):
                acc_copy(half, chunk).wait_send()

        @pl.when((col if half == 0 else last - col) < last)
        def _():
            for part in range(2):
                for source in range(2):
                    for place in range(QUARTERS):
                        z_copy(half, part, source, place).wait_send()

    @pl.when(is_end)
    def _():
        for part in range(2):
            for place in range(QUARTERS):
                stage_copy(part, place).wait_send()


def chain(last, activations, gain, weights, squares, taps):
    tokens, features = activations.shape
    rows = FILTER_LEN
    pieces = tokens // rows
    chunks = 4 * pieces
    width = weights[0].shape[0] // 4
    dma = pltpu.SemaphoreType.DMA
    vmem = pl.BlockSpec(memory_space=pltpu.VMEM)
    hbm = pl.BlockSpec(memory_space=pl.ANY)
    return pl.pallas_call(
        functools.partial(chain_kernel, last),
        in_specs=[vmem, vmem, hbm, hbm, hbm, vmem, vmem],
        out_specs=vmem,
        out_shape=jax.ShapeDtypeStruct((tokens, 8 * width), jnp.bfloat16),
        scratch_shapes=[
            pltpu.VMEM((2, pieces, rows, features), jnp.bfloat16),
            pltpu.VMEM((4, 3 * width, features), jnp.bfloat16),
            pltpu.VMEM((4, features, 3 * width), jnp.bfloat16),
            pltpu.VMEM((2, chunks, rows, 3 * width), jnp.bfloat16),
            pltpu.VMEM(taps.shape, jnp.float32),
            pltpu.VMEM((2 * (last + 1),) + squares.shape, jnp.float32),
            pltpu.VMEM((2, 3, SUB + rows, width), jnp.float32),
            pltpu.VMEM((2, SUB + rows, width), jnp.float32),
            pltpu.VMEM((2, SUB, 2 * rows, width), jnp.float32),
            pltpu.VMEM((2, tokens, width), jnp.bfloat16),
            pltpu.VMEM((2, 2, 2, tokens, width), jnp.bfloat16),
            dma((4, 3)), dma, dma, dma((2, 2)), dma((2 * (last + 1),)),
            dma((2, chunks)), dma((2, chunks)), dma((pieces,)), dma((pieces,)),
            dma((2, QUARTERS)), dma((2, QUARTERS)), dma((2, 2, 2, QUARTERS)), dma((2, 2, 2, QUARTERS)),
        ],
        compiler_params=pltpu.CompilerParams(
            collective_id=0, has_side_effects=True, vmem_limit_bytes=44 * 2**20
        ),
    )(activations, gain, *weights, squares, taps)


def on_device_chain(
    n_col, activations, norm_gain, w_query, w_key, w_value, short_taps, long_taps, skip_gain, w_out
):
    held = w_query.shape[0]
    width = held // 4
    group = short_taps.shape[2]

    taps = jnp.concatenate(
        [short_taps.reshape(9, group), skip_gain[None], jnp.zeros((6, group), jnp.float32), long_taps], axis=0
    )
    taps = jnp.transpose(taps.reshape(-1, 2, width), (1, 0, 2))

    w_full = lax.all_gather(w_out, "ctx", axis=0, tiled=True)
    w_full = jnp.transpose(w_full.reshape(-1, 2, 4, width), (0, 2, 1, 3)).reshape(w_full.shape)

    as_float = activations.astype(jnp.float32)
    squares = jnp.sum(as_float * as_float, axis=1).reshape(-1, FILTER_LEN)

    block_rows = chain(n_col - 1, activations, norm_gain[None], (w_query, w_key, w_value), squares, taps)
    out_part = lax.dot_general(
        block_rows, w_full, (((1,), (1,)), ((), ())), preferred_element_type=jnp.float32
    )
    return lax.psum_scatter(out_part.astype(jnp.bfloat16), "row", scatter_dimension=0, tiled=True)


def solution(mesh):
    in_specs = (
        P("ctx", "col"),
        P("col"),
        P(("row", "ctx"), "col"),
        P(("row", "ctx"), "col"),
        P(("row", "ctx"), "col"),
        P(None, None, ("row", "col")),
        P(None, ("row", "col")),
        P(("row", "col")),
        P(("col", "ctx"), "row"),
    )
    out_specs = P(("ctx", "row"), "col")
    n_ctx, n_row, n_col = mesh.shape["ctx"], mesh.shape["row"], mesh.shape["col"]
    if n_ctx == 2 and n_col == 4:
        body = functools.partial(on_device_chain, n_col)
    else:
        body = functools.partial(on_device, n_ctx, n_row, n_col)
    return jax.shard_map(body, mesh=mesh, in_specs=in_specs, out_specs=out_specs, check_vma=False)
```

```python
import functools

import jax
import jax.numpy as jnp
from jax import lax
from jax.experimental import pallas as pl
from jax.experimental.pallas import tpu as pltpu
from jax.sharding import PartitionSpec as P

D = 4096
SHORT_LEN = 3
FILTER_LEN = 128
SUB = 8
epsilon = 1e-05


def filter_kernel(x_ref, scale_ref, short_ref, long_ref, skip_ref, out_ref, prev, gates, shifted):
    step = pl.program_id(0)
    rows = x_ref.shape[1]

    @pl.when(step == 0)
    def _():
        prev[...] = jnp.zeros_like(prev)
        gates[0:SUB, :] = jnp.zeros((SUB, gates.shape[1]), jnp.float32)
        shifted[:, 0:FILTER_LEN, :] = jnp.zeros((SUB, FILTER_LEN, shifted.shape[2]), jnp.float32)

    @pl.when(step > 0)
    def _():
        shifted[:, 0:FILTER_LEN, :] = shifted[:, rows : rows + FILTER_LEN, :]

    filtered = []
    for which in range(3):
        now = x_ref[which].astype(jnp.float32) * scale_ref[...]
        prev[which, SUB:, :] = now
        total = short_ref[which, 0:1, :] * now
        for tap in range(1, SHORT_LEN):
            total = total + short_ref[which, tap : tap + 1, :] * prev[which, SUB - tap : SUB - tap + rows, :]
        filtered.append(total)
        prev[which, 0:SUB, :] = prev[which, rows : rows + SUB, :]
    gate = filtered[1] * filtered[2]
    gates[SUB:, :] = gate
    for move in range(SUB):
        shifted[move, FILTER_LEN:, :] = gates[SUB - move : SUB - move + rows, :]
    gates[0:SUB, :] = gates[rows : rows + SUB, :]
    total = skip_ref[...] * gate
    for move in range(SUB):
        for back in range(0, FILTER_LEN, SUB):
            total = total + long_ref[back + move : back + move + 1, :] * shifted[
                move, FILTER_LEN - back : FILTER_LEN - back + rows, :
            ]
    out_ref[...] = (filtered[0] * total).astype(out_ref.dtype)


def mix(stacked, scale, short_taps, long_taps, skip_gain):
    _, tokens, channels = stacked.shape
    rows = FILTER_LEN
    return pl.pallas_call(
        filter_kernel,
        grid=(tokens // rows,),
        in_specs=[
            pl.BlockSpec((3, rows, channels), lambda i: (0, i, 0)),
            pl.BlockSpec((rows, 1), lambda i: (i, 0)),
            pl.BlockSpec((3, SHORT_LEN, channels), lambda i: (0, 0, 0)),
            pl.BlockSpec((FILTER_LEN, channels), lambda i: (0, 0)),
            pl.BlockSpec((1, channels), lambda i: (0, 0)),
        ],
        out_specs=pl.BlockSpec((rows, channels), lambda i: (i, 0)),
        out_shape=jax.ShapeDtypeStruct((tokens, channels), jnp.bfloat16),
        scratch_shapes=[
            pltpu.VMEM((3, SUB + rows, channels), jnp.float32),
            pltpu.VMEM((SUB + rows, channels), jnp.float32),
            pltpu.VMEM((SUB, FILTER_LEN + rows, channels), jnp.float32),
        ],
    )(stacked, scale, short_taps, long_taps, skip_gain)


def shift(value, axis, size, by):
    return lax.ppermute(value, axis, [((i + by) % size, i) for i in range(size)])


def on_device(
    n_ctx, n_row, n_col,
    activations, norm_gain, w_query, w_key, w_value, short_taps, long_taps, skip_gain, w_out,
):
    ctx, col = lax.axis_index("ctx"), lax.axis_index("col")
    tokens, features = activations.shape
    held = w_query.shape[0]
    width = held // n_col
    stacked = jnp.stack([w_query, w_key, w_value]).reshape(3, n_col, width, features)

    taps = jnp.concatenate([short_taps.reshape(9, -1), long_taps, skip_gain[None]], axis=0)
    taps = lax.all_gather(taps, "col", axis=1, tiled=True)
    taps = lax.dynamic_slice_in_dim(taps, ctx * held + col * width, width, 1)

    w_full = lax.all_gather(w_out, "ctx", axis=0, tiled=True)
    w_full = jnp.transpose(w_full.reshape(-1, n_ctx, n_col, width), (0, 2, 1, 3)).reshape(w_full.shape)

    qkv = jnp.zeros((3, n_ctx * tokens, width), jnp.bfloat16)
    squares = jnp.zeros((n_ctx * tokens,), jnp.float32)
    for step in range(n_ctx):
        part = activations if step == 0 else shift(activations, "ctx", n_ctx, step)
        first = lax.rem(ctx + step, n_ctx) * tokens
        as_float = part.astype(jnp.float32)
        squares = lax.dynamic_update_slice(squares, jnp.sum(as_float * as_float, axis=1), (first,))
        scaled = (as_float * norm_gain).astype(jnp.bfloat16)
        partial_value = jnp.einsum("td,skcd->kstc", scaled, stacked, preferred_element_type=jnp.float32)
        summed = lax.psum_scatter(partial_value.astype(jnp.bfloat16), "col", scatter_dimension=0, tiled=True)
        qkv = lax.dynamic_update_slice(qkv, summed[0], (0, first, 0))

    total = squares.reshape(-1, 128)
    for step in range(1, n_col):
        total = total + shift(squares.reshape(-1, 128), "col", n_col, step)
    scale = lax.rsqrt(total / D + epsilon).reshape(-1, 1)

    mixed = mix(qkv, scale, taps[:9].reshape(3, 3, width), taps[9:-1], taps[-1:])

    spread = lax.all_to_all(
        mixed.reshape(n_ctx, tokens, width), "ctx", split_axis=0, concat_axis=0, tiled=True
    )
    spread = jnp.transpose(spread, (1, 0, 2)).reshape(tokens, n_ctx * width)
    block_rows = lax.all_gather(spread, "col", axis=1, tiled=True)
    out_part = lax.dot_general(
        block_rows, w_full, (((1,), (1,)), ((), ())), preferred_element_type=jnp.float32
    )
    return lax.psum_scatter(out_part.astype(jnp.bfloat16), "row", scatter_dimension=0, tiled=True)


QUARTERS = 4
SLACK = 2
LATE = 2
BLOCKS = 2


def chain_kernel(
    last, x_ref, gain_ref, wq_ref, wk_ref, wv_ref, squares_ref, own_taps, out_ref,
    xs, w_rows, w_ref, acc, taps_ref, totals, prev, gates, shifted, stage, gath,
    w_sem, taps_send, taps_recv, sq_send, sq_recv,
    acc_send, acc_recv, x_send, x_recv, stage_send, stage_recv, z_send, z_recv,
):
    ctx, col = lax.axis_index("ctx"), lax.axis_index("col")
    pieces = xs.shape[1]
    chunks = acc.shape[1]
    rows = xs.shape[2]
    width = gath.shape[4]
    quarter = gath.shape[3] // QUARTERS
    group_len = pieces // BLOCKS
    n_col = last + 1
    is_end = (col == 0) | (col == last)
    end_half = jnp.where(col == 0, 0, 1)
    left, right = jnp.maximum(col - 1, 0), jnp.minimum(col + 1, last)
    peer = {"ctx": 1 - ctx}
    mesh_ids = pl.DeviceIdType.MESH

    def w_copy(group, which):
        source = (wq_ref, wk_ref, wv_ref)[which]
        return pltpu.make_async_copy(
            source.at[pl.ds(group * width, width)], w_rows.at[group, pl.ds(which * width, width)],
            w_sem.at[group, which],
        )

    for group in range(4):
        for which in range(3):
            w_copy(group, which).start()

    barrier = pltpu.get_barrier_semaphore()
    for far in range(2):
        for away in range(n_col):
            if far or away:
                other = {"ctx": lax.rem(ctx + far, 2), "col": lax.rem(col + away, n_col)}
                pl.semaphore_signal(barrier, inc=1, device_id=other, device_id_type=mesh_ids)

    xs[0] = (x_ref[...].astype(jnp.float32) * gain_ref[...]).astype(jnp.bfloat16).reshape(xs.shape[1:])
    pl.semaphore_wait(barrier, 2 * n_col - 1)

    def x_copy(piece):
        return pltpu.make_async_remote_copy(
            xs.at[0, piece], xs.at[1, piece], x_send.at[piece], x_recv.at[piece],
            device_id=peer, device_id_type=mesh_ids,
        )

    def acc_copy(half, chunk):
        return pltpu.make_async_remote_copy(
            acc.at[half, chunk], acc.at[half, chunk], acc_send.at[half, chunk], acc_recv.at[half, chunk],
            device_id={"col": left if half == 0 else right}, device_id_type=mesh_ids,
        )

    def stage_copy(part, place):
        rows_of = pl.ds(pl.multiple_of(place * quarter, quarter), quarter)
        return pltpu.make_async_remote_copy(
            stage.at[part, rows_of], gath.at[end_half, part, ctx, rows_of],
            stage_send.at[part, place], stage_recv.at[part, place],
            device_id=peer, device_id_type=mesh_ids,
        )

    def z_copy(half, part, source, place):
        rows_of = pl.ds(pl.multiple_of(place * quarter, quarter), quarter)
        return pltpu.make_async_remote_copy(
            gath.at[half, part, source, rows_of], gath.at[half, part, source, rows_of],
            z_send.at[half, part, source, place], z_recv.at[half, part, source, place],
            device_id={"col": right if half == 0 else left}, device_id_type=mesh_ids,
        )

    def sq_copy(far, away):
        me = ctx * n_col + col
        return pltpu.make_async_remote_copy(
            squares_ref, totals.at[me], sq_send.at[far, 0 if away == 0 else 1], sq_recv.at[me],
            device_id={"ctx": lax.rem(ctx + far, 2), "col": away}, device_id_type=mesh_ids,
        )

    taps_owner = col // 2 == ctx
    taps_end = lax.rem(col, 2) * last
    taps_copy = pltpu.make_async_remote_copy(
        own_taps, taps_ref, taps_send, taps_recv, device_id={"col": taps_end}, device_id_type=mesh_ids
    )

    for far in range(2):
        for away in (0, last):
            @pl.when((col != away) if far == 0 else (col >= 0))
            def _():
                sq_copy(far, away).start()

    @pl.when(taps_owner & (taps_end != col))
    def _():
        taps_copy.start()

    @pl.when(taps_owner & (taps_end == col))
    def _():
        taps_ref[...] = own_taps[...]

    @pl.when(is_end)
    def _():
        totals[ctx * n_col + col] = squares_ref[...]

    for group in range(4):
        for which in range(3):
            w_copy(group, which).wait()

    @pl.loop(0, 4)
    def _(group):
        w_ref[group] = jnp.transpose(w_rows[group])

    def wait_small():
        for source in range(2 * n_col):
            @pl.when(source != ctx * n_col + col)
            def _():
                pltpu.make_async_remote_copy(
                    squares_ref, totals.at[source], sq_send.at[0, 0], sq_recv.at[source],
                    device_id=peer, device_id_type=mesh_ids,
                ).wait_recv()

        @pl.when(jnp.logical_not(taps_owner & (taps_end == col)))
        def _():
            taps_copy.wait_recv()

        for half in range(2):
            total = totals[half * n_col]
            for source in range(1, n_col):
                total = total + totals[half * n_col + source]
            totals[half * n_col] = lax.rsqrt(total / D + epsilon)

    diagonal = lax.broadcasted_iota(jnp.int32, (rows, rows), 0) == lax.broadcasted_iota(
        jnp.int32, (rows, rows), 1
    )

    def filter_block(part, mine, place, again):
        chunk = mine * 2 * group_len + part * group_len + place // BLOCKS
        held = pl.ds(pl.multiple_of(lax.rem(place, BLOCKS) * rows, rows), rows)
        half = lax.rem(ctx + mine, 2)
        row_scale = totals[half * n_col, pl.ds(place, 1), :]
        scale = jnp.sum(jnp.where(diagonal, row_scale, 0.0), axis=1, keepdims=True)
        taps = taps_ref.at[part]

        @pl.when((place == 0) & ((mine == 0) | (ctx == 1)) & jnp.logical_not(again))
        def _():
            prev[part] = jnp.zeros(prev.shape[1:], jnp.float32)
            gates[part, 0:SUB, :] = jnp.zeros((SUB, width), jnp.float32)
            shifted[part, :, rows:, :] = jnp.zeros((SUB, rows, width), jnp.float32)

        shifted[part, :, 0:rows, :] = shifted[part, :, rows:, :]
        filtered = []
        for which in range(3):
            now = acc[end_half, chunk, held, which * width : (which + 1) * width].astype(jnp.float32) * scale
            prev[part, which, SUB:, :] = now
            total = taps[3 * which : 3 * which + 1, :] * now
            for tap in range(1, SHORT_LEN):
                row = 3 * which + tap
                total = total + taps[row : row + 1, :] * prev[part, which, SUB - tap : SUB - tap + rows, :]
            filtered.append(total)
            prev[part, which, 0:SUB, :] = prev[part, which, rows : rows + SUB, :]
        gate = filtered[1] * filtered[2]
        gates[part, SUB:, :] = gate
        for move in range(SUB):
            shifted[part, move, rows:, :] = gates[part, SUB - move : SUB - move + rows, :]
        gates[part, 0:SUB, :] = gates[part, rows : rows + SUB, :]
        total = taps[9:10, :] * gate
        for move in range(SUB):
            window = shifted[part, move]
            for back in range(0, FILTER_LEN, SUB):
                row = 16 + back + move
                total = total + taps[row : row + 1, :] * window[rows - back : 2 * rows - back, :]
        value = (filtered[0] * total).astype(jnp.bfloat16)
        spot = pl.ds(pl.multiple_of(place * rows, rows), rows)

        @pl.when(mine == 0)
        def _():
            gath[end_half, part, ctx, spot, :] = value

        @pl.when(mine == 1)
        def _():
            stage[part, spot, :] = value

    def pass_on(half, hops, part, source, place, from_peer):
        @pl.when(hops > 0)
        def _():
            z_copy(half, part, source, place).wait_recv()

        if from_peer:
            @pl.when(hops == 0)
            def _():
                stage_copy(part, place).wait_recv()

        @pl.when(hops < last)
        def _():
            z_copy(half, part, source, place).start()

    @pl.loop(0, chunks + 2 * SLACK * last)
    def _(step):
        @pl.when(step < group_len)
        def _():
            for block in range(BLOCKS):
                x_copy(step * BLOCKS + block).start()

        first = step - SLACK * jnp.minimum(col, last - col)

        @pl.when((first >= 2 * group_len) & (first < 3 * group_len))
        def _():
            for block in range(BLOCKS):
                x_copy((first - 2 * group_len) * BLOCKS + block).wait_recv()

        for half in range(2):
            hops = last - col if half == 0 else col
            chunk = step - SLACK * hops

            @pl.when((chunk >= 0) & (chunk < chunks))
            def _():
                part = lax.rem(chunk // group_len, 2)

                @pl.when(hops > 0)
                def _():
                    acc_copy(half, chunk).wait_recv()

                @pl.loop(0, BLOCKS)
                def _(block):
                    place = lax.rem(chunk, group_len) * BLOCKS + block
                    held = pl.ds(pl.multiple_of(block * rows, rows), rows)
                    own = lax.dot_general(
                        xs[chunk // (2 * group_len), place], w_ref[2 * half + part],
                        (((1,), (0,)), ((), ())), preferred_element_type=jnp.float32,
                    )

                    @pl.when(hops == 0)
                    def _():
                        acc[half, chunk, held, :] = own.astype(jnp.bfloat16)

                    @pl.when(hops > 0)
                    def _():
                        held_sum = acc[half, chunk, held, :].astype(jnp.float32)
                        acc[half, chunk, held, :] = (own + held_sum).astype(jnp.bfloat16)

                @pl.when(hops < last)
                def _():
                    acc_copy(half, chunk).start()

        done = step - SLACK * last

        @pl.when(is_end & (done == 0))
        def _():
            wait_small()

        @pl.when(is_end & (done >= 0) & (done < chunks))
        def _():
            mine, part = done // (2 * group_len), lax.rem(done // group_len, 2)
            place = lax.rem(done, group_len)
            seam = (mine == 1) & (place == group_len - 1) & (ctx == 1)

            @pl.loop(0, BLOCKS + jnp.where(seam, 1, 0))
            def _(block):
                again = block == BLOCKS
                filter_block(
                    part, jnp.where(again, 0, mine), jnp.where(again, 0, place * BLOCKS + block), again
                )

            @pl.when(mine == 1)
            def _():
                stage_copy(part, place).start()

        for half in range(2):
            hops = col if half == 0 else last - col
            event = step - SLACK * (last + hops)

            @pl.when((event >= 0) & (event < 2 * group_len))
            def _():
                place = lax.rem(event, QUARTERS)

                @pl.when((ctx == 0) | (place > 0))
                def _():
                    pass_on(half, hops, event // QUARTERS, ctx, place, False)

            @pl.when((event >= 2 * group_len + LATE) & (event < chunks))
            def _():
                late = event - 2 * group_len - LATE
                pass_on(half, hops, late // QUARTERS, 1 - ctx, lax.rem(late, QUARTERS), True)

            @pl.when((event == 3 * group_len) & (ctx == 1))
            def _():
                pass_on(half, hops, 0, ctx, 0, False)

    for half in range(2):
        hops = col if half == 0 else last - col
        @pl.when(ctx == 1)
        def _():
            pass_on(half, hops, 1, ctx, 0, False)

    for place in range(QUARTERS - LATE, QUARTERS):
        for half in range(2):
            pass_on(half, col if half == 0 else last - col, 1, 1 - ctx, place, True)

    for half in range(2):
        for part in range(2):
            for source in range(2):
                place = (half * 2 + part) * 2 + source
                out_ref[:, place * width : (place + 1) * width] = gath[half, part, source]

    @pl.loop(0, pieces)
    def _(piece):
        x_copy(piece).wait_send()

    for far in range(2):
        for away in (0, last):
            @pl.when((col != away) if far == 0 else (col >= 0))
            def _():
                sq_copy(far, away).wait_send()

    @pl.when(taps_owner & (taps_end != col))
    def _():
        taps_copy.wait_send()

    for half in range(2):
        @pl.when((last - col if half == 0 else col) < last)
        def _():
            @pl.loop(0, chunks)
            def _(chunk):
                acc_copy(half, chunk).wait_send()

        @pl.when((col if half == 0 else last - col) < last)
        def _():
            for part in range(2):
                for source in range(2):
                    for place in range(QUARTERS):
                        z_copy(half, part, source, place).wait_send()

    @pl.when(is_end)
    def _():
        for part in range(2):
            for place in range(QUARTERS):
                stage_copy(part, place).wait_send()


def chain(last, activations, gain, weights, squares, taps):
    tokens, features = activations.shape
    rows = FILTER_LEN
    pieces = tokens // rows
    chunks = 4 * pieces // BLOCKS
    width = weights[0].shape[0] // 4
    dma = pltpu.SemaphoreType.DMA
    vmem = pl.BlockSpec(memory_space=pltpu.VMEM)
    hbm = pl.BlockSpec(memory_space=pl.ANY)
    return pl.pallas_call(
        functools.partial(chain_kernel, last),
        in_specs=[vmem, vmem, hbm, hbm, hbm, vmem, vmem],
        out_specs=vmem,
        out_shape=jax.ShapeDtypeStruct((tokens, 8 * width), jnp.bfloat16),
        scratch_shapes=[
            pltpu.VMEM((2, pieces, rows, features), jnp.bfloat16),
            pltpu.VMEM((4, 3 * width, features), jnp.bfloat16),
            pltpu.VMEM((4, features, 3 * width), jnp.bfloat16),
            pltpu.VMEM((2, chunks, BLOCKS * rows, 3 * width), jnp.bfloat16),
            pltpu.VMEM(taps.shape, jnp.float32),
            pltpu.VMEM((2 * (last + 1),) + squares.shape, jnp.float32),
            pltpu.VMEM((2, 3, SUB + rows, width), jnp.float32),
            pltpu.VMEM((2, SUB + rows, width), jnp.float32),
            pltpu.VMEM((2, SUB, 2 * rows, width), jnp.float32),
            pltpu.VMEM((2, tokens, width), jnp.bfloat16),
            pltpu.VMEM((2, 2, 2, tokens, width), jnp.bfloat16),
            dma((4, 3)), dma, dma, dma((2, 2)), dma((2 * (last + 1),)),
            dma((2, chunks)), dma((2, chunks)), dma((pieces,)), dma((pieces,)),
            dma((2, QUARTERS)), dma((2, QUARTERS)), dma((2, 2, 2, QUARTERS)), dma((2, 2, 2, QUARTERS)),
        ],
        compiler_params=pltpu.CompilerParams(
            collective_id=0, has_side_effects=True, vmem_limit_bytes=44 * 2**20
        ),
    )(activations, gain, *weights, squares, taps)


def on_device_chain(
    n_col, activations, norm_gain, w_query, w_key, w_value, short_taps, long_taps, skip_gain, w_out
):
    held = w_query.shape[0]
    width = held // 4
    group = short_taps.shape[2]

    taps = jnp.concatenate(
        [short_taps.reshape(9, group), skip_gain[None], jnp.zeros((6, group), jnp.float32), long_taps], axis=0
    )
    taps = jnp.transpose(taps.reshape(-1, 2, width), (1, 0, 2))

    w_full = lax.all_gather(w_out, "ctx", axis=0, tiled=True)
    w_full = jnp.transpose(w_full.reshape(-1, 2, 4, width), (0, 2, 1, 3)).reshape(w_full.shape)

    as_float = activations.astype(jnp.float32)
    squares = jnp.sum(as_float * as_float, axis=1).reshape(-1, FILTER_LEN)

    block_rows = chain(n_col - 1, activations, norm_gain[None], (w_query, w_key, w_value), squares, taps)
    out_part = lax.dot_general(
        block_rows, w_full, (((1,), (1,)), ((), ())), preferred_element_type=jnp.float32
    )
    return lax.psum_scatter(out_part.astype(jnp.bfloat16), "row", scatter_dimension=0, tiled=True)


def solution(mesh):
    in_specs = (
        P("ctx", "col"),
        P("col"),
        P(("row", "ctx"), "col"),
        P(("row", "ctx"), "col"),
        P(("row", "ctx"), "col"),
        P(None, None, ("row", "col")),
        P(None, ("row", "col")),
        P(("row", "col")),
        P(("col", "ctx"), "row"),
    )
    out_specs = P(("ctx", "row"), "col")
    n_ctx, n_row, n_col = mesh.shape["ctx"], mesh.shape["row"], mesh.shape["col"]
    if n_ctx == 2 and n_col == 4:
        body = functools.partial(on_device_chain, n_col)
    else:
        body = functools.partial(on_device, n_ctx, n_row, n_col)
    return jax.shard_map(body, mesh=mesh, in_specs=in_specs, out_specs=out_specs, check_vma=False)
```
